32 devices in a mesh: gx: 4 (over z), gy: 8 (over y, x, core).
Axes of the slice: x: 2, y: 2, z: 4, core: 2. Of those that a mesh axis runs over, the one named last changes fastest.
Arguments:
- observed: bfloat16 [1024, 1024, 128], P('gx', 'gy'), may hold values from -6 to 6
- confidence: bfloat16 [1024, 1024, 128], P('gx', 'gy'), may hold values from 0.1 to 13
- iterate: float32 [1024, 1024, 128], P('gx', 'gy'), may hold values from -24 to 24
- kernel_bank: float32 [3, 64], replicated, may hold values from 0.02 to 1
- tap_index: int32 [3, 33], replicated, may hold values from 0 to 63
- offsets: int32 [3], replicated, may hold values from -4 to 4
- basis_x: bfloat16 [1024, 1024], P('gx'), may hold values from -0.1875 to 0.1875
- basis_y: bfloat16 [1024, 1024], P('gy'), may hold values from -0.1875 to 0.1875
- basis_z: bfloat16 [128, 128], replicated, may hold values from -0.5 to 0.5
- eigen_x: float32 [1024], P('gx'), may hold values from 0.1 to 1
- eigen_y: float32 [1024], replicated, may hold values from 0.1 to 1
- eigen_z: float32 [128], replicated, may hold values from 0.1 to 1
Outputs:
- updated: float32 [1024, 1024, 128], P('gx', 'gy')
- residual: float32 [1024, 1024, 128], P('gx', 'gy')
The draws below stay inside these ranges and needn't reach their ends.
All inputs are finite; a program needn't handle non-finite values.
Results may differ from the reference program's by a relative error of at most 0.0028.
Values may be sent and summed in bfloat16 or wider, within the bound.
A program may use at most 256 MiB of HBM per device.

```python
import math
import jax
import jax.numpy as jnp
from jax import lax

NX = 1024
NY = 1024
NZ = 128
HALF = 16
SHIFT = 4
BANK = 64
TAPS = 33


def draw_confidence(key, part):
    sub_key = jax.random.fold_in(key, 11)
    x_frac = (jnp.arange(NX, dtype=jnp.float32) / NX)[:, None, None]
    y_frac = (jnp.arange(NY, dtype=jnp.float32) / NY)[None, :, None]
    baseline = jnp.exp(jax.random.uniform(sub_key, (NX, NY, NZ), jnp.float32, jnp.log(0.1), 0.0))
    slope = 2.0
    growth = (1.0 + slope * x_frac) * (1.0 + slope * y_frac)
    return (baseline * growth).astype(jnp.bfloat16)


def draw_offsets(key, part):
    shuffle = jax.random.permutation(jax.random.fold_in(key, 5), 3)
    baseline = jax.random.randint(jax.random.fold_in(key, 7), (3,), -SHIFT, SHIFT + 1)
    axis_ids = jnp.arange(3, dtype=jnp.int32)
    chosen = jnp.where(axis_ids == shuffle[1], -SHIFT, baseline)
    return jnp.where(axis_ids == shuffle[0], SHIFT, chosen).astype(jnp.int32)


def place_ends(drawn, stream_key, least, top_value):
    extent = drawn.shape
    spot = [jax.random.randint(jax.random.fold_in(stream_key, axis), (), 0, extent[axis]) for axis in range(len(extent))]
    drawn = drawn.at[tuple(spot)].set(least)
    longest = extent.index(max(extent))
    spot[longest] = (spot[longest] + 1) % extent[longest]
    return drawn.at[tuple(spot)].set(top_value)


def levels(stream_key, dims, split, low, largest):
    loudness = 1.0
    for position, blocks in split:
        steps = jax.random.uniform(jax.random.fold_in(jax.random.fold_in(stream_key, 6), position), (blocks,), jnp.float32, low / len(split), largest / len(split))
        loudness = loudness * jnp.repeat(jnp.exp(steps), dims[position] // blocks).reshape((-1,) + (1,) * (len(dims) - 1 - position))
    return loudness


def normal_values(rng, dims, width, reach, pieces=(), held_as=jnp.bfloat16):
    result = width * jax.random.normal(rng, dims, jnp.float32)
    if pieces:
        result = result * levels(rng, dims, pieces, -0.22, 0.18)
    return jnp.clip(result, -reach, reach).astype(held_as)


def setup_inputs(seed: int = 0) -> dict:
    splits = jax.random.split(jax.random.key(seed), 13)
    observed = normal_values(splits[0], (NX, NY, NZ), 1.0, 6.0, ((0, 4), (1, 8)))
    confidence = draw_confidence(jax.random.fold_in(splits[12], 71), 0)
    iterate = normal_values(splits[2], (NX, NY, NZ), 4.0, 24.0, ((0, 4), (1, 8)), jnp.float32)
    kernel_bank = jnp.clip(jnp.exp(jax.random.uniform(splits[3], (3, BANK), jnp.float32, math.log(0.02), math.log(1.0))), 0.02, 1.0)
    tap_index = place_ends(jax.random.randint(splits[4], (3, TAPS), 0, BANK), jax.random.fold_in(splits[4], 1), 0, BANK - 1).astype(jnp.int32)
    offsets = draw_offsets(jax.random.fold_in(splits[12], 71), 0)
    basis_x = normal_values(splits[6], (NX, NX), NX ** -0.5, 0.1875, ((0, 4),))
    basis_y = normal_values(splits[7], (NY, NY), NY ** -0.5, 0.1875, ((0, 8),))
    basis_z = normal_values(splits[8], (NZ, NZ), NZ ** -0.5, 0.5)
    eigen_x = jnp.clip(jnp.exp(math.log(1.0) - 2.3025851 * jax.random.uniform(splits[9], (NX,), jnp.float32) ** levels(splits[9], (NX,), ((0, 4),), -0.2, 0.2)), 0.1, 1.0)
    eigen_y = jnp.clip(jnp.exp(jax.random.uniform(splits[10], (NY,), jnp.float32, math.log(0.1), math.log(1.0))), 0.1, 1.0)
    eigen_z = jnp.clip(jnp.exp(jax.random.uniform(splits[11], (NZ,), jnp.float32, math.log(0.1), math.log(1.0))), 0.1, 1.0)
    return {"observed": observed, "confidence": confidence, "iterate": iterate, "kernel_bank": kernel_bank, "tap_index": tap_index, "offsets": offsets, "basis_x": basis_x, "basis_y": basis_y, "basis_z": basis_z, "eigen_x": eigen_x, "eigen_y": eigen_y, "eigen_z": eigen_z}


highest = lax.Precision.HIGHEST
tikhonov = 0.002


def kernels_of(kernel_bank, tap_index):
    raw_taps = jnp.take_along_axis(kernel_bank, tap_index, axis=1)
    return raw_taps / jnp.sum(raw_taps, axis=1, keepdims=True)


def shift_blur(source, kernel, offset, axis_pos):
    rim_width = HALF + SHIFT
    pad_spec = [(0, 0), (0, 0), (0, 0)]
    pad_spec[axis_pos] = (rim_width, rim_width)
    padded = jnp.pad(source, pad_spec)
    length = source.shape[axis_pos]
    accum = jnp.zeros_like(source)
    for tap_pos in range(2 * HALF + 1):
        begin_at = (offset + (rim_width + tap_pos - HALF)).astype(jnp.int32)
        accum = accum + kernel[tap_pos] * lax.dynamic_slice_in_dim(padded, begin_at, length, axis_pos)
    return accum


def blur_all(source, kernels, offsets):
    along_z = shift_blur(source, kernels[2], offsets[2], 2)
    along_x = shift_blur(along_z, kernels[0], offsets[0], 0)
    return shift_blur(along_x, kernels[1], offsets[1], 1)


def precondition(gradient, basis_x, basis_y, basis_z, eigen_x, eigen_y, eigen_z):
    basis_xf = basis_x.astype(jnp.float32)
    basis_yf = basis_y.astype(jnp.float32)
    basis_zf = basis_z.astype(jnp.float32)
    gradient_b = gradient.astype(jnp.bfloat16).astype(jnp.float32)
    section_one = jnp.einsum('xyz,zk->xyk', gradient_b, basis_zf, precision=highest).astype(jnp.bfloat16)
    section_two = jnp.einsum('xyz,xk->kyz', section_one.astype(jnp.float32), basis_xf, precision=highest).astype(jnp.bfloat16)
    section_three = jnp.einsum('xyz,yk->xkz', section_two.astype(jnp.float32), basis_yf, precision=highest)
    inverse = 1.0 / (eigen_x[:, None, None] * eigen_y[None, :, None] * eigen_z[None, None, :] + tikhonov)
    section_four = (section_three * inverse).astype(jnp.bfloat16)
    section_five = jnp.einsum('xkz,jk->xjz', section_four.astype(jnp.float32), basis_yf, precision=highest).astype(jnp.bfloat16)
    section_six = jnp.einsum('kyz,jk->jyz', section_five.astype(jnp.float32), basis_xf, precision=highest).astype(jnp.bfloat16)
    return jnp.einsum('xyk,zk->xyz', section_six.astype(jnp.float32), basis_zf, precision=highest)


def reference(observed, confidence, iterate, kernel_bank, tap_index, offsets, basis_x, basis_y, basis_z, eigen_x, eigen_y, eigen_z):
    kernels = kernels_of(kernel_bank, tap_index)
    weights = confidence.astype(jnp.float32)
    misfit = observed.astype(jnp.float32) - blur_all(iterate, kernels, offsets)
    gradient = blur_all(weights * misfit, kernels[:, ::-1], -offsets) - tikhonov * iterate
    direction = precondition(gradient, basis_x, basis_y, basis_z, eigen_x, eigen_y, eigen_z)
    descent = jnp.sum(gradient * direction)
    blurred = blur_all(direction, kernels, offsets)
    energy = jnp.sum(weights * blurred * blurred) + tikhonov * jnp.sum(direction * direction)
    step_size = descent / energy
    return iterate + step_size * direction, misfit - step_size * blurred
```

```python
import jax
import jax.numpy as jnp
from jax import lax
from jax.sharding import PartitionSpec as P

HALF = 16
SHIFT = 4
CHUNKS = 2


highest = lax.Precision.HIGHEST
tikhonov = 0.002


def exchange(block, axis, dim, width):
    count = lax.axis_size(axis)
    forward = [(i, i + 1) for i in range(count - 1)]
    backward = [(target, source) for source, target in forward]
    low = lax.ppermute(
        lax.slice_in_dim(block, block.shape[dim] - width, None, axis=dim), axis, forward
    )
    high = lax.ppermute(lax.slice_in_dim(block, 0, width, axis=dim), axis, backward)
    return low, high


def kernels_of(kernel_bank, tap_index):
    entries = jnp.arange(kernel_bank.shape[1], dtype=jnp.int32)
    chosen = tap_index[:, :, None] == entries[None, None, :]
    raw_taps = jnp.sum(jnp.where(chosen, kernel_bank[:, None, :], 0.0), axis=2)
    return raw_taps / jnp.sum(raw_taps, axis=1, keepdims=True)


def band_matrix(kernel, offset, out_count, in_count, margin):
    center = (kernel.shape[0] - 1) // 2
    row_pos = lax.broadcasted_iota(jnp.int32, (out_count, in_count), 0)
    col_pos = lax.broadcasted_iota(jnp.int32, (out_count, in_count), 1)
    position = col_pos - row_pos - margin + center - offset
    tap_ids = jnp.arange(kernel.shape[0], dtype=jnp.int32)
    chosen = position[None, :, :] == tap_ids[:, None, None]
    return jnp.sum(jnp.where(chosen, kernel[:, None, None], 0.0), axis=0)


def split_dot(spec, matrix, block):
    return jnp.einsum(spec, matrix, block.astype(jnp.float32), precision=lax.Precision.HIGH)


def turned(array, axis_name, dim, sign):
    count = lax.axis_size(axis_name)
    size = array.shape[dim] // count
    mine = lax.axis_index(axis_name)
    pieces = [
        lax.dynamic_slice_in_dim(array, lax.rem(mine + sign * step + count, count) * size, size, dim)
        for step in range(count)
    ]
    return jnp.concatenate(pieces, axis=dim)


def swap(block, axis_name, split, concat, sign):
    count = lax.axis_size(axis_name)
    pieces = jnp.split(block, count, axis=split)
    arrived = [pieces[0]]
    for step in range(1, count):
        pairs = [(i, (i + sign * step) % count) for i in range(count)]
        arrived.append(lax.ppermute(pieces[step], axis_name, pairs))
    return jnp.concatenate(arrived, axis=concat)


def blur_xy(along_z, kernels, offsets):
    rim = HALF + SHIFT
    block_x, block_y, _ = along_z.shape
    x_matrix = band_matrix(kernels[0], offsets[0], block_x, block_x + 2 * rim, rim)
    y_matrix = band_matrix(kernels[1], offsets[1], block_y, block_y + 2 * rim, rim)
    low, high = exchange(along_z, "gx", 0, rim)
    extended = jnp.concatenate([low, along_z, high], axis=0)
    along_x = split_dot("ic,cyz->iyz", x_matrix, extended).astype(jnp.bfloat16)
    low, high = exchange(along_x, "gy", 1, rim)
    inner = split_dot("jc,xcz->xjz", y_matrix[:, rim:-rim], along_x)
    rims = jnp.concatenate([low, high], axis=1)
    rim_matrix = jnp.concatenate([y_matrix[:, :rim], y_matrix[:, -rim:]], axis=1)
    return inner + split_dot("jc,xcz->xjz", rim_matrix, rims)


def apply_blur(source, kernels, offsets):
    depth = source.shape[2]
    z_matrix = band_matrix(kernels[2], offsets[2], depth, depth, 0)
    along_z = jnp.einsum("xyc,zc->xyz", source, z_matrix, precision=lax.Precision.HIGH)
    return blur_xy(along_z.astype(jnp.bfloat16), kernels, offsets)


def shards(
    observed,
    confidence,
    iterate,
    kernel_bank,
    tap_index,
    offsets,
    basis_x,
    basis_y,
    basis_z,
    eigen_x,
    eigen_y,
    eigen_z,
):
    kernels = kernels_of(kernel_bank, tap_index)
    adjoint_kernels = kernels[:, ::-1]
    weights = confidence.astype(jnp.float32)
    misfit = observed.astype(jnp.float32) - apply_blur(iterate, kernels, offsets)
    gradient = apply_blur(weights * misfit, adjoint_kernels, -offsets) - tikhonov * iterate
    full_x = lax.all_gather(basis_x, "gx", axis=0, tiled=True)
    full_y = lax.all_gather(basis_y, "gy", axis=0, tiled=True)

    gradient_b = gradient.astype(jnp.bfloat16)
    gx_size = lax.axis_size("gx")
    depth = basis_z.shape[0]
    share_z = depth // gx_size
    chunks = min(CHUNKS, share_z)
    part = share_z // chunks
    z_ahead = turned(basis_z, "gx", 1, 1).reshape(depth, gx_size, chunks, part)
    eigen_part = lax.dynamic_slice_in_dim(eigen_z, lax.axis_index("gx") * share_z, share_z)
    all_x = lax.all_gather(eigen_x, "gx", axis=0, tiled=True)
    share_x = all_x.shape[0] // lax.axis_size("gy")
    part_x = lax.dynamic_slice_in_dim(all_x, lax.axis_index("gy") * share_x, share_x)
    x_rows_behind = turned(full_x, "gx", 0, -1)
    x_ahead = turned(x_rows_behind, "gy", 1, 1)
    x_return = turned(turned(full_x, "gx", 0, 1), "gy", 1, -1)
    y_behind = turned(full_y, "gy", 0, -1)
    y_ahead = turned(full_y, "gy", 0, 1)
    found = []
    for chunk in range(chunks):
        modes = z_ahead[:, :, chunk].reshape(depth, gx_size * part)
        section_one = jnp.einsum(
            "zk,xyz->kxy", modes, gradient_b, preferred_element_type=jnp.float32
        ).astype(jnp.bfloat16)
        lines = swap(section_one, "gx", 0, 1, 1)
        section_two = jnp.einsum(
            "xj,kxy->kjy", x_ahead, lines, preferred_element_type=jnp.float32
        ).astype(jnp.bfloat16)
        lines = swap(section_two, "gy", 1, 2, 1)
        part_z = eigen_part[chunk * part : (chunk + 1) * part]
        inverse = 1.0 / (
            part_x[None, :, None] * eigen_y[None, None, :] * part_z[:, None, None] + tikhonov
        )
        section_four = (
            jnp.einsum("axy,yk->axk", lines, y_behind, preferred_element_type=jnp.float32)
            * inverse
        ).astype(jnp.bfloat16)
        section_five = jnp.einsum(
            "axk,jk->axj", section_four, y_ahead, preferred_element_type=jnp.float32
        ).astype(jnp.bfloat16)
        lines = swap(section_five, "gy", 2, 1, 1)
        section_six = jnp.einsum(
            "jx,kxy->kjy", x_return, lines, preferred_element_type=jnp.float32
        ).astype(jnp.bfloat16)
        found.append(swap(section_six, "gx", 1, 0, 1))
    section_six = jnp.concatenate(found, axis=0)
    basis_z = (
        turned(basis_z, "gx", 1, -1)
        .reshape(depth, gx_size, chunks, part)
        .transpose(0, 2, 1, 3)
        .reshape(depth, depth)
    )
    direction = jnp.einsum("kxy,zk->xyz", section_six, basis_z, preferred_element_type=jnp.float32)
    z_matrix = band_matrix(kernels[2], offsets[2], depth, depth, 0)
    z_modes = jnp.dot(z_matrix, basis_z.astype(jnp.float32), precision=highest)
    along_z = jnp.einsum(
        "kxy,zk->xyz", section_six.astype(jnp.float32), z_modes, precision=lax.Precision.HIGH
    ).astype(jnp.bfloat16)
    local_descent = jnp.sum(gradient * direction)
    descent = lax.psum(local_descent, ("gx", "gy"))
    blurred = blur_xy(along_z, kernels, offsets)
    data_sum, norm_sum = lax.psum(
        (jnp.sum(weights * blurred * blurred), jnp.sum(direction * direction)), ("gx", "gy")
    )
    energy = data_sum + tikhonov * norm_sum
    step_size = descent / energy
    return (iterate + step_size * direction, misfit - step_size * blurred)


def solution(mesh):
    return jax.shard_map(
        shards,
        mesh=mesh,
        in_specs=(
            P("gx", "gy", None),
            P("gx", "gy", None),
            P("gx", "gy", None),
            P(),
            P(),
            P(),
            P("gx", None),
            P("gy", None),
            P(),
            P("gx"),
            P(),
            P(),
        ),
        out_specs=(P("gx", "gy", None), P("gx", "gy", None)),
        check_vma=False,
    )
```

```python
import jax
import jax.numpy as jnp
from jax import lax
from jax.sharding import PartitionSpec as P

HALF = 16
SHIFT = 4
CHUNKS = 4


highest = lax.Precision.HIGHEST
tikhonov = 0.002


def exchange(block, axis, dim, width):
    count = lax.axis_size(axis)
    forward = [(i, i + 1) for i in range(count - 1)]
    backward = [(target, source) for source, target in forward]
    low = lax.ppermute(
        lax.slice_in_dim(block, block.shape[dim] - width, None, axis=dim), axis, forward
    )
    high = lax.ppermute(lax.slice_in_dim(block, 0, width, axis=dim), axis, backward)
    return low, high


def kernels_of(kernel_bank, tap_index):
    entries = jnp.arange(kernel_bank.shape[1], dtype=jnp.int32)
    chosen = tap_index[:, :, None] == entries[None, None, :]
    raw_taps = jnp.sum(jnp.where(chosen, kernel_bank[:, None, :], 0.0), axis=2)
    return raw_taps / jnp.sum(raw_taps, axis=1, keepdims=True)


def band_matrix(kernel, offset, out_count, in_count, margin):
    center = (kernel.shape[0] - 1) // 2
    row_pos = lax.broadcasted_iota(jnp.int32, (out_count, in_count), 0)
    col_pos = lax.broadcasted_iota(jnp.int32, (out_count, in_count), 1)
    position = col_pos - row_pos - margin + center - offset
    tap_ids = jnp.arange(kernel.shape[0], dtype=jnp.int32)
    chosen = position[None, :, :] == tap_ids[:, None, None]
    return jnp.sum(jnp.where(chosen, kernel[:, None, None], 0.0), axis=0)


def split_dot(spec, matrix, block):
    return jnp.einsum(spec, matrix, block.astype(jnp.float32), precision=lax.Precision.HIGH)


def turned(array, axis_name, dim, sign):
    count = lax.axis_size(axis_name)
    size = array.shape[dim] // count
    mine = lax.axis_index(axis_name)
    pieces = [
        lax.dynamic_slice_in_dim(array, lax.rem(mine + sign * step + count, count) * size, size, dim)
        for step in range(count)
    ]
    return jnp.concatenate(pieces, axis=dim)


def swap(block, axis_name, split, concat, sign):
    count = lax.axis_size(axis_name)
    pieces = jnp.split(block, count, axis=split)
    arrived = [pieces[0]]
    for step in range(1, count):
        pairs = [(i, (i + sign * step) % count) for i in range(count)]
        arrived.append(lax.ppermute(pieces[step], axis_name, pairs))
    return jnp.concatenate(arrived, axis=concat)


def blur_xy(along_z, kernels, offsets):
    rim = HALF + SHIFT
    block_x, block_y, _ = along_z.shape
    x_matrix = band_matrix(kernels[0], offsets[0], block_x, block_x + 2 * rim, rim)
    y_matrix = band_matrix(kernels[1], offsets[1], block_y, block_y + 2 * rim, rim)
    low, high = exchange(along_z, "gx", 0, rim)
    extended = jnp.concatenate([low, along_z, high], axis=0)
    along_x = split_dot("ic,cyz->iyz", x_matrix, extended).astype(jnp.bfloat16)
    low, high = exchange(along_x, "gy", 1, rim)
    spread = jnp.broadcast_to(y_matrix, (block_x,) + y_matrix.shape)
    inner = split_dot("xjc,xcz->xjz", spread[:, :, rim:-rim], along_x)
    rims = jnp.concatenate([low, high], axis=1)
    rim_matrix = jnp.concatenate([spread[:, :, :rim], spread[:, :, -rim:]], axis=2)
    return inner + split_dot("xjc,xcz->xjz", rim_matrix, rims)


def apply_blur(source, kernels, offsets):
    depth = source.shape[2]
    z_matrix = band_matrix(kernels[2], offsets[2], depth, depth, 0)
    along_z = jnp.einsum("xyc,zc->xyz", source, z_matrix, precision=lax.Precision.HIGH)
    return blur_xy(along_z.astype(jnp.bfloat16), kernels, offsets)


def shards(
    observed,
    confidence,
    iterate,
    kernel_bank,
    tap_index,
    offsets,
    basis_x,
    basis_y,
    basis_z,
    eigen_x,
    eigen_y,
    eigen_z,
):
    kernels = kernels_of(kernel_bank, tap_index)
    adjoint_kernels = kernels[:, ::-1]
    weights = confidence.astype(jnp.float32)
    misfit = observed.astype(jnp.float32) - apply_blur(iterate, kernels, offsets)
    gradient = apply_blur(weights * misfit, adjoint_kernels, -offsets) - tikhonov * iterate
    full_x = lax.all_gather(basis_x, "gx", axis=0, tiled=True)
    full_y = lax.all_gather(basis_y, "gy", axis=0, tiled=True)

    gradient_b = gradient.astype(jnp.bfloat16)
    gx_size = lax.axis_size("gx")
    depth = basis_z.shape[0]
    share_z = depth // gx_size
    chunks = min(CHUNKS, share_z)
    part = share_z // chunks
    z_ahead = turned(basis_z, "gx", 1, 1).reshape(depth, gx_size, chunks, part)
    eigen_part = lax.dynamic_slice_in_dim(eigen_z, lax.axis_index("gx") * share_z, share_z)
    all_x = lax.all_gather(eigen_x, "gx", axis=0, tiled=True)
    share_x = all_x.shape[0] // lax.axis_size("gy")
    part_x = lax.dynamic_slice_in_dim(all_x, lax.axis_index("gy") * share_x, share_x)
    x_rows_behind = turned(full_x, "gx", 0, -1)
    x_ahead = turned(x_rows_behind, "gy", 1, 1)
    x_return = turned(turned(full_x, "gx", 0, 1), "gy", 1, -1)
    y_behind = turned(full_y, "gy", 0, -1)
    y_ahead = turned(full_y, "gy", 0, 1)
    found = []
    for chunk in range(chunks):
        modes = z_ahead[:, :, chunk].reshape(depth, gx_size * part)
        section_one = jnp.einsum(
            "zk,xyz->kxy", modes, gradient_b, preferred_element_type=jnp.float32
        ).astype(jnp.bfloat16)
        lines = swap(section_one, "gx", 0, 1, 1)
        section_two = jnp.einsum(
            "xj,kxy->kjy", x_ahead, lines, preferred_element_type=jnp.float32
        ).astype(jnp.bfloat16)
        lines = swap(section_two, "gy", 1, 2, 1)
        part_z = eigen_part[chunk * part : (chunk + 1) * part]
        inverse = 1.0 / (
            part_x[None, :, None] * eigen_y[None, None, :] * part_z[:, None, None] + tikhonov
        )
        section_four = (
            jnp.einsum("axy,yk->axk", lines, y_behind, preferred_element_type=jnp.float32)
            * inverse
        ).astype(jnp.bfloat16)
        section_five = jnp.einsum(
            "axk,jk->axj", section_four, y_ahead, preferred_element_type=jnp.float32
        ).astype(jnp.bfloat16)
        lines = swap(section_five, "gy", 2, 1, 1)
        section_six = jnp.einsum(
            "jx,kxy->kjy", x_return, lines, preferred_element_type=jnp.float32
        ).astype(jnp.bfloat16)
        found.append(swap(section_six, "gx", 1, 0, 1))
    section_six = jnp.concatenate(found, axis=0)
    basis_z = (
        turned(basis_z, "gx", 1, -1)
        .reshape(depth, gx_size, chunks, part)
        .transpose(0, 2, 1, 3)
        .reshape(depth, depth)
    )
    direction = jnp.einsum("kxy,zk->xyz", section_six, basis_z, preferred_element_type=jnp.float32)
    z_matrix = band_matrix(kernels[2], offsets[2], depth, depth, 0)
    z_modes = jnp.dot(z_matrix, basis_z.astype(jnp.float32), precision=highest)
    along_z = jnp.einsum(
        "kxy,zk->xyz", section_six.astype(jnp.float32), z_modes, precision=lax.Precision.HIGH
    ).astype(jnp.bfloat16)
    blurred = blur_xy(along_z, kernels, offsets)
    local = jnp.stack(
        [
            jnp.sum(gradient * direction),
            jnp.sum(weights * blurred * blurred) + tikhonov * jnp.sum(direction * direction),
        ]
    )
    descent, energy = jnp.sum(lax.all_gather(local, ("gx", "gy")), axis=0)
    step_size = descent / energy
    return (iterate + step_size * direction, misfit - step_size * blurred)


def solution(mesh):
    return jax.shard_map(
        shards,
        mesh=mesh,
        in_specs=(
            P("gx", "gy", None),
            P("gx", "gy", None),
            P("gx", "gy", None),
            P(),
            P(),
            P(),
            P("gx", None),
            P("gy", None),
            P(),
            P("gx"),
            P(),
            P(),
        ),
        out_specs=(P("gx", "gy", None), P("gx", "gy", None)),
        check_vma=False,
    )
```
